32 devices in a mesh: grp: 2 (over y), tile: 4 (over z), lev: 2 (over x), sub: 2 (over core).
Axes of the slice: x: 2, y: 2, z: 4, core: 2. Of those that a mesh axis runs over, the one named last changes fastest.
Arguments:
- control: bfloat16 [2048, 64, 192], P('tile', 'lev', ('grp', 'sub')), parts along dimension 2, may hold values from -6 to 6
- node_count: int32 [4], P('tile'), may hold values from 256 to 512, as said below
- vert_coef: bfloat16 [64, 64], replicated
- send_list: int32 [4, 4, 1], replicated, may hold values from 0 to 1
- conv_slots: int32 [4, 2, 9], P('tile'), may hold values from 0 to 5, as said below
- conv_coef: bfloat16 [4, 2, 9, 256, 256], P('tile'), may hold values from -0.125 to 0.125
- interp_slots: int32 [8, 3, 3], P('tile'), may hold values from 0 to 5
- interp_coef: bfloat16 [8, 3, 3, 256, 256], P(('tile', 'sub')), may hold values from -0.21875 to 0.21875
Outputs:
- model_field: bfloat16 [6144, 64, 192], P(('tile', 'sub'), 'lev', 'grp'), parts along dimension 2
The draws below stay inside these ranges and needn't reach their ends.
There are 2 independent parts, one for each index of `grp`. The reference program is written for one: setup_inputs(seed, part) draws one part's arguments, and reference() takes and returns one part's arrays. A program takes and returns all parts, laid end to end along the dimension named above; an argument that names none is the same for every part. Nothing has to cross between parts.
Inputs may be any that keep to these rules, and one draw needn't show every extreme that they name: `node_count`: some tile holds 512 valid nodes in every draw. `conv_slots`: entry k = 0 is the block's own local block; every lent entry of a tile's list is read by some block of that tile.
All inputs are finite; a program needn't handle non-finite values.
Results may differ from the reference program's by a relative error of at most 0.02.
Values may be sent and summed in bfloat16 or wider, within the bound.
No kernel may reach another device: no remote copies, remote signals or barrier semaphores. Data moves between devices by JAX's collectives and lax.ppermute only.
A program may use at most 64 MiB of HBM per device.

```python
import jax
import jax.numpy as jnp
from jax import lax

BLK = 256
NB = 2
K = 9
HB = 1
PB = 3
J = 3
LEVELS = 64
MEM = 96
NODES = 2048
POINTS = 6144
EXT = 6
N_TILE = 4
N_LEV = 2
N_SUB = 2


def draw_node_count(key, part):
    key = jax.random.fold_in(key, 3)
    first, second = jax.random.split(key)
    most = NB * BLK
    counts = jax.random.randint(first, (N_TILE,), most // 2, most + 1)
    fullest = jax.random.randint(second, (), 0, N_TILE)
    return jnp.where(jnp.arange(N_TILE) == fullest, most, counts).astype(jnp.int32)


def draw_vert_coef(key, part):
    key = jax.random.fold_in(key, 5)
    reach = 2.0 * (LEVELS // N_LEV)
    rows = jnp.arange(LEVELS, dtype=jnp.float32)[:, None]
    cols = jnp.arange(LEVELS, dtype=jnp.float32)[None, :]
    factor = jax.random.uniform(key, (LEVELS, LEVELS), jnp.float32, 0.5, 1.5)
    values = jnp.exp(-jnp.abs(rows - cols) / reach) * factor / jnp.sqrt(reach)
    return values.astype(jnp.bfloat16)


def draw_conv_slots(key, part):
    key = jax.random.fold_in(key, 7)
    keys = jax.random.split(key, N_TILE)
    lent = N_TILE * HB

    def one_tile(tile_key):
        order = jax.random.permutation(tile_key, lent)
        block = jnp.arange(NB, dtype=jnp.int32)[:, None]
        slot = jnp.arange(K, dtype=jnp.int32)[None, :]
        place = (block * (K - 1) + slot - 1) % lent
        far = NB + order[place]
        return jnp.where(slot == 0, block, far).astype(jnp.int32)
    return jax.vmap(one_tile)(keys)


def plant(values, key, smallest, largest):
    spot = [jax.random.randint(jax.random.fold_in(key, axis), (), 0, length) for axis, length in enumerate(values.shape)]
    main_axis = values.shape.index(max(values.shape))
    next_to = spot[:main_axis] + [(spot[main_axis] + 1) % values.shape[main_axis]] + spot[main_axis + 1:]
    return values.at[tuple(spot)].set(smallest).at[tuple(next_to)].set(largest)


def block_levels(rng, shape, pieces, least, top_value):
    level = 1.0
    for position, shards_of in pieces:
        steps = jax.random.uniform(jax.random.fold_in(jax.random.fold_in(rng, 6), position), (shards_of,), jnp.float32, least / len(pieces), top_value / len(pieces))
        level = level * jnp.repeat(jnp.exp(steps), shape[position] // shards_of).reshape((-1,) + (1,) * (len(shape) - 1 - position))
    return level


def noise(rng, dims, scale, bound, cuts=(), held_as=jnp.bfloat16):
    array = scale * jax.random.normal(rng, dims, jnp.float32)
    if cuts:
        array = array * block_levels(rng, dims, cuts, -0.22, 0.18)
    return jnp.clip(array, -bound, bound).astype(held_as)


def setup_inputs(seed: int = 0, part: int = 0) -> dict:
    seeds = jax.random.split(jax.random.key(seed), 9)
    own_keys = jax.random.split(jax.random.fold_in(seeds[8], part), 9)
    control = noise(own_keys[0], (NODES, LEVELS, MEM), 1.0, 6.0, ((0, 4), (1, 2), (2, 2)))
    node_count = draw_node_count(jax.random.fold_in(seeds[8], 71), part)
    vert_coef = draw_vert_coef(jax.random.fold_in(seeds[8], 71), part)
    send_list = plant(jax.random.randint(seeds[3], (N_TILE, N_TILE, HB), 0, NB), jax.random.fold_in(seeds[3], 1), 0, NB - 1).astype(jnp.int32)
    conv_slots = draw_conv_slots(jax.random.fold_in(seeds[8], 71), part)
    conv_coef = noise(seeds[5], (N_TILE, NB, K, BLK, BLK), (K * BLK) ** -0.5, 0.125, ((0, 4),))
    interp_slots = plant(jax.random.randint(seeds[6], (N_TILE * N_SUB, PB, J), 0, EXT), jax.random.fold_in(seeds[6], 1), 0, EXT - 1).astype(jnp.int32)
    interp_coef = noise(seeds[7], (N_TILE * N_SUB, PB, J, BLK, BLK), (J * BLK) ** -0.5, 0.21875, ((0, 8),))
    return dict(control=control, node_count=node_count, vert_coef=vert_coef, send_list=send_list, conv_slots=conv_slots, conv_coef=conv_coef, interp_slots=interp_slots, interp_coef=interp_coef)


def reference(control, node_count, vert_coef, send_list, conv_slots, conv_coef, interp_slots, interp_coef):
    tile_nodes = NB * BLK
    index = jnp.arange(NODES, dtype=jnp.int32)
    valid = (index % tile_nodes) < node_count[index // tile_nodes]
    masked = jnp.where(valid[:, None, None], control, jnp.zeros_like(control))
    level_rows = LEVELS // N_LEV

    def add_part(place, total):
        start = jnp.asarray(place).astype(jnp.int32) * level_rows
        weights = lax.dynamic_slice_in_dim(vert_coef, start, level_rows, 1).astype(jnp.float32)
        layers = lax.dynamic_slice_in_dim(masked, start, level_rows, 1).astype(jnp.float32)
        part = jnp.einsum("al,nlm->nam", weights, layers, precision=lax.Precision.HIGHEST)
        return total + lax.optimization_barrier(part.astype(jnp.bfloat16)).astype(jnp.float32)

    total = lax.fori_loop(0, N_LEV, add_part, jnp.zeros((NODES, LEVELS, MEM), jnp.float32))
    vertical = total.astype(jnp.bfloat16)
    columns = LEVELS * MEM
    flat = vertical.reshape(N_TILE * NB, BLK, columns)
    tiles = jnp.arange(N_TILE, dtype=jnp.int32)
    lent = jnp.transpose(send_list, (1, 0, 2)) + (tiles * NB)[None, :, None]
    lent = lent.reshape(N_TILE, N_TILE * HB)
    own = tiles[:, None] * NB + jnp.arange(NB, dtype=jnp.int32)[None, :]
    ext_ids = jnp.concatenate([own, lent], 1).astype(jnp.int32)

    def spread_tile(tile):
        ids = ext_ids[tile][conv_slots[tile]]
        chosen = flat[ids].astype(jnp.float32)
        spread = jnp.einsum("bkij,bkjc->bic", conv_coef[tile].astype(jnp.float32), chosen, precision=lax.Precision.HIGHEST)
        return spread.astype(jnp.bfloat16)

    spread_all = lax.map(spread_tile, tiles).reshape(N_TILE * NB, BLK, columns)

    def interp_row(row):
        ids = ext_ids[row // N_SUB][interp_slots[row]]
        picked = spread_all[ids].astype(jnp.float32)
        result = jnp.einsum("pjab,pjbc->pac", interp_coef[row].astype(jnp.float32), picked, precision=lax.Precision.HIGHEST)
        return result.astype(jnp.bfloat16)

    field = lax.map(interp_row, jnp.arange(N_TILE * N_SUB, dtype=jnp.int32))
    return field.reshape(POINTS, LEVELS, MEM)
```

```python
import functools

import jax
import jax.numpy as jnp
from jax import lax
from jax.experimental import pallas as pl
from jax.experimental.pallas import tpu as pltpu
from jax.sharding import PartitionSpec as P

CHUNK = 16
VMEM_LIMIT = 48 * 1024 * 1024
SMEM = pl.BlockSpec(memory_space=pltpu.SMEM)
VMEM = pl.BlockSpec(memory_space=pltpu.VMEM)
HBM = pl.BlockSpec(memory_space=pl.ANY)
BF16 = jnp.bfloat16
F32 = jnp.float32


def params():
    return pltpu.CompilerParams(vmem_limit_bytes=VMEM_LIMIT)


def dot_nt(a, b):
    return lax.dot_general(a, b, (((1,), (1,)), ((), ())), preferred_element_type=F32)


def merge_kernel(tiles, place, send, slots, coef, out, total):
    blocks, taps = coef.shape[:2]
    own = blocks
    t = place[0]
    total[...] = jnp.zeros_like(total)
    for b in range(blocks):
        for k in range(taps):
            slot = slots[0, b, k]
            lender = jnp.maximum(slot - own, 0)
            distance = lax.rem(t - lender + tiles, tiles)
            lent = jnp.where(distance == 0, send[lender, t, 0], own - 1 + distance)
            entry = jnp.where(slot < own, slot, lent)
            total[b, entry] += coef[b, k].astype(F32)
    out[...] = total[...].astype(BF16)


def weight_kernel(levels, place, vert, out):
    rows = levels * CHUNK
    total = vert.shape[0]
    lev = place[1]
    shape = (rows, total)
    pick = lax.broadcasted_iota(jnp.int32, shape, 0) // CHUNK + lev * levels
    left = (lax.broadcasted_iota(jnp.int32, shape, 1) == pick).astype(BF16)
    spread = jnp.dot(left, vert[...], preferred_element_type=F32).astype(BF16)
    row = lax.broadcasted_iota(jnp.int32, (rows, rows), 0)
    col = lax.broadcasted_iota(jnp.int32, (rows, rows), 1)
    same = lax.rem(row, CHUNK) == lax.rem(col, CHUNK)
    for side in range(2):
        base = jnp.where(lev == side, 0, levels)
        wanted = lax.broadcasted_iota(jnp.int32, shape, 0) // CHUNK + base
        right = (lax.broadcasted_iota(jnp.int32, shape, 1) == wanted).astype(BF16)
        full = dot_nt(spread, right)
        out[side] = jnp.where(same, full, 0.0).astype(BF16)


def vertical_kernel(count, weight, own, other, out):
    value = jnp.dot(weight[0], own[...], preferred_element_type=F32)
    value += jnp.dot(weight[1], other[...], preferred_element_type=F32)
    node = lax.broadcasted_iota(jnp.int32, value.shape, 1)
    value = jnp.where(node < count[0], value, 0.0).astype(BF16)
    size = out.shape[-1]
    for b in range(out.shape[0]):
        out[b] = value[:, b * size : (b + 1) * size]


def spread_kernel(tiles, place, send, coef_own, coef_lent, own, *rest):
    rights, lefts = rest[: tiles - 1], rest[tiles - 1 : 2 * tiles - 2]
    out, held, sems = rest[2 * tiles - 2 :]
    t = place[0]
    blocks = own.shape[0]
    copies = [pltpu.make_async_copy(own, held.at[0], sems.at[0])]
    copies[0].start()
    for d in range(1, tiles):
        from_left = t >= d

        @pl.when(from_left)
        def _():
            pltpu.make_async_copy(rights[d - 1], held.at[d], sems.at[d]).start()

        @pl.when(jnp.logical_not(from_left))
        def _():
            pltpu.make_async_copy(lefts[tiles - d - 1], held.at[d], sems.at[d]).start()

        copies.append(pltpu.make_async_copy(rights[d - 1], held.at[d], sems.at[d]))
    for copy in copies:
        copy.wait()
    for j in range(blocks + tiles - 1):
        away = max(0, j - blocks + 1)
        source = lax.rem(t - away + tiles, tiles)
        total = None
        for e in range(blocks + tiles - 1):
            hop = max(0, e - blocks + 1)
            lender = lax.rem(source - hop + tiles, tiles)
            if e < blocks:
                block = e
            else:
                block = send[lender, source, 0]
            distance = lax.rem(t - lender + tiles, tiles)
            if j < blocks:
                matrix = coef_own[j, e]
            else:
                matrix = coef_lent[:, away - 1, e].reshape(coef_own.shape[-2:])
            part = dot_nt(held[distance, block], matrix)
            total = part if total is None else total + part
        out[j] = total.astype(BF16)


def interp_kernel(tiles, place, send, slots, coef, field, *rest):
    out = rest[-1]
    own = field.shape[0] - tiles + 1
    t, sub = place[0], place[2]
    p = pl.program_id(0)
    total = None
    for j in range(coef.shape[2]):
        slot = slots[sub, p, j]
        lender = jnp.maximum(slot - own, 0)
        distance = lax.rem(t - lender + tiles, tiles)
        lent = jnp.where(distance == 0, send[lender, t, 0], own - 1 + distance)
        entry = jnp.where(slot < own, slot, lent)
        part = dot_nt(field[entry], coef[0, 0, j])
        total = part if total is None else total + part
    out[...] = total.astype(BF16).reshape(out.shape)


def interpolate(chunk, half, tiles, place, send, slots, coef, field, shape, before):
    levels, members, points = shape
    count = coef.shape[1]
    chunks = members // 2 // CHUNK
    size = coef.shape[-1]

    def place_out(p, place, send, slots):
        sub = place[2]
        side = sub if half == 0 else 1 - sub
        return (0, side * chunks + chunk, p)

    in_specs = [
        pl.BlockSpec((1, 1) + coef.shape[2:], lambda p, *_: (0, p, 0, 0, 0)),
        pl.BlockSpec(field.shape, lambda p, *_: (0, 0, 0)),
    ]
    operands = [coef, field]
    aliases = {}
    if before is not None:
        in_specs.append(HBM)
        operands.append(before)
        aliases = {5: 0}
    return pl.pallas_call(
        functools.partial(interp_kernel, tiles),
        grid_spec=pltpu.PrefetchScalarGridSpec(
            num_scalar_prefetch=3,
            grid=(count,),
            in_specs=in_specs,
            out_specs=pl.BlockSpec((levels, CHUNK, size), place_out),
        ),
        out_shape=jax.ShapeDtypeStruct(shape, BF16),
        input_output_aliases=aliases,
        compiler_params=params(),
        name="interpolate",
    )(place, send, slots, *operands)


def local(
    control, node_count, vert_coef, send_list, conv_slots, conv_coef, interp_slots, interp_coef
):
    nodes, levels, members = control.shape
    _, blocks, taps, size, _ = conv_coef.shape
    tiles = lax.axis_size("tile")
    halves = lax.axis_size("sub")
    points = interp_coef.shape[1] * size
    t, lev, sub, grp = (lax.axis_index(n) for n in ("tile", "lev", "sub", "grp"))
    place = jnp.stack([t, lev, sub]).astype(jnp.int32)
    chunks = members // CHUNK
    rows = levels * CHUNK
    entries = blocks + tiles - 1
    swap = [(0, 1), (1, 0)]
    right = [(i, i + 1) for i in range(tiles - 1)]
    left = [(i + 1, i) for i in range(tiles - 1)]

    state = control.transpose(1, 2, 0)
    mine = [state[:, c * CHUNK : (c + 1) * CHUNK].reshape(rows, nodes) for c in range(chunks)]
    theirs = [lax.ppermute(x, "lev", swap) for x in mine]

    merged = pl.pallas_call(
        functools.partial(merge_kernel, tiles),
        in_specs=[SMEM, SMEM, SMEM, VMEM],
        out_specs=VMEM,
        out_shape=jax.ShapeDtypeStruct((blocks, entries, size, size), BF16),
        scratch_shapes=[pltpu.VMEM((blocks, entries, size, size), F32)],
        compiler_params=params(),
        name="merge_taps",
    )(place, send_list, conv_slots, conv_coef[0])

    shares = lax.axis_size("grp") * lax.axis_size("lev") * halves
    share = (grp * lax.axis_size("lev") + lev) * halves + sub
    part = size // shares
    pieces = []
    for d in range(1, tiles):
        target = lax.rem(t + d, tiles)
        block = send_list[t, target, 0]
        piece = lax.dynamic_slice(
            merged, (block, 0, share * part, 0), (1, entries, part, size)
        )[0]
        ring = [(i, (i + d) % tiles) for i in range(tiles)]
        pieces.append(lax.ppermute(piece, "tile", ring))
    coef_lent = lax.all_gather(jnp.stack(pieces), ("grp", "lev", "sub"))

    weight = pl.pallas_call(
        functools.partial(weight_kernel, levels),
        in_specs=[SMEM, VMEM],
        out_specs=VMEM,
        out_shape=jax.ShapeDtypeStruct((2, rows, rows), BF16),
        compiler_params=params(),
        name="level_weights",
    )(place, vert_coef)

    result = None
    for c in range(chunks):
        vertical = pl.pallas_call(
            vertical_kernel,
            in_specs=[SMEM, VMEM, VMEM, VMEM],
            out_specs=VMEM,
            out_shape=jax.ShapeDtypeStruct((blocks, rows, size), BF16),
            compiler_params=params(),
            name="vertical",
        )(node_count, weight, mine[c], theirs[c])
        rights, lefts = [vertical], [vertical]
        for hop in range(tiles - 1):
            rights.append(lax.ppermute(rights[-1], "tile", right[hop:]))
            lefts.append(lax.ppermute(lefts[-1], "tile", left[: tiles - 1 - hop]))
        fields = pl.pallas_call(
            functools.partial(spread_kernel, tiles),
            in_specs=[SMEM, SMEM, VMEM, VMEM] + [HBM] * (2 * tiles - 1),
            out_specs=VMEM,
            out_shape=jax.ShapeDtypeStruct((entries, rows, size), BF16),
            scratch_shapes=[
                pltpu.VMEM((tiles, blocks, rows, size), BF16),
                pltpu.SemaphoreType.DMA((tiles,)),
            ],
            compiler_params=params(),
            name="spread",
        )(place, send_list, merged, coef_lent, vertical, *rights[1:], *lefts[1:])
        other = lax.ppermute(fields, "sub", swap)
        shape = (levels, halves * members, points)
        for half, field in enumerate((fields, other)):
            result = interpolate(
                c, half, tiles, place, send_list, interp_slots, interp_coef, field, shape, result
            )
    return result.transpose(2, 0, 1)


def plain(
    control, node_count, vert_coef, send_list, conv_slots, conv_coef, interp_slots, interp_coef
):
    node_rows, level_rows, member_rows = control.shape
    block_len = conv_coef.shape[-1]
    block_count = conv_coef.shape[1]
    columns = level_rows * member_rows
    tile_count = lax.axis_size("tile")
    halves = lax.axis_size("sub")
    tile_place = lax.axis_index("tile")
    level_place = lax.axis_index("lev")
    half_place = lax.axis_index("sub")
    position = lax.broadcasted_iota(jnp.int32, (node_rows, 1, 1), 0)
    masked = jnp.where(position < node_count[0], control, jnp.zeros_like(control))
    own_weights = lax.dynamic_slice_in_dim(vert_coef, level_place * level_rows, level_rows, 1)
    partial_value = jnp.einsum(
        "al,nlm->nam", own_weights, masked, preferred_element_type=jnp.float32
    )
    vertical = lax.psum_scatter(
        partial_value.astype(jnp.bfloat16), "lev", scatter_dimension=1, tiled=True
    )
    blocks = vertical.reshape(block_count, block_len, columns)
    incoming_ids = lax.dynamic_index_in_dim(send_list, tile_place, 1, keepdims=False)
    source_base = (jnp.arange(tile_count, dtype=jnp.int32) * block_count)[:, None]
    everything = lax.all_gather(blocks, "tile", axis=0, tiled=True)
    received = everything[source_base + incoming_ids]
    extended = jnp.concatenate([blocks, received.reshape(-1, block_len, columns)], 0)
    chosen = extended[conv_slots[0]]
    spread = jnp.einsum(
        "bkij,bkjc->bic", conv_coef[0], chosen, preferred_element_type=jnp.float32
    ).astype(jnp.bfloat16)
    spread_every = lax.all_gather(spread, "tile", axis=0, tiled=True)
    spread_lent = spread_every[source_base + incoming_ids]
    spread_ext = jnp.concatenate([spread, spread_lent.reshape(-1, block_len, columns)], 0)
    own_slots = lax.dynamic_index_in_dim(interp_slots, half_place, 0, keepdims=False)
    members_all = lax.all_gather(spread_ext, "sub", axis=2, tiled=True)
    picked = members_all[own_slots]
    result = jnp.einsum(
        "pjab,pjbc->pac", interp_coef[0], picked, preferred_element_type=jnp.float32
    )
    point_rows = result.shape[0] * block_len
    shaped = result.reshape(point_rows, halves, level_rows, member_rows)
    return (
        shaped.transpose(0, 2, 1, 3)
        .reshape(point_rows, level_rows, halves * member_rows)
        .astype(jnp.bfloat16)
    )


def solution(mesh):
    placed = (
        P("tile", "lev", ("grp", "sub")),
        P("tile"),
        P(),
        P(),
        P("tile", None, None),
        P("tile", None, None, None, None),
        P("tile", None, None),
        P(("tile", "sub"), None, None, None, None),
    )
    short = mesh.shape["tile"] <= 4 and mesh.shape["lev"] == 2 and mesh.shape["sub"] == 2
    return jax.shard_map(
        local if short else plain,
        mesh=mesh,
        in_specs=placed,
        out_specs=P(("tile", "sub"), "lev", "grp"),
        check_vma=False,
    )
```

```python
import functools

import jax
import jax.numpy as jnp
from jax import lax
from jax.experimental import pallas as pl
from jax.experimental.pallas import tpu as pltpu
from jax.sharding import PartitionSpec as P

CHUNK = 16
VMEM_LIMIT = 20 * 1024 * 1024
SMEM = pl.BlockSpec(memory_space=pltpu.SMEM)
VMEM = pl.BlockSpec(memory_space=pltpu.VMEM)
HBM = pl.BlockSpec(memory_space=pl.ANY)
BF16 = jnp.bfloat16
F32 = jnp.float32


def params():
    return pltpu.CompilerParams(vmem_limit_bytes=VMEM_LIMIT)


def after(value, *others):
    return lax.optimization_barrier((value, others))[0]


def dot_nt(a, b):
    return lax.dot_general(a, b, (((1,), (1,)), ((), ())), preferred_element_type=F32)


def merge_kernel(tiles, place, send, slots, coef, out, total):
    blocks, taps = coef.shape[:2]
    own = blocks
    t = place[0]
    total[...] = jnp.zeros_like(total)
    for b in range(blocks):
        for k in range(taps):
            slot = slots[0, b, k]
            lender = jnp.maximum(slot - own, 0)
            distance = t ^ lender
            lent = jnp.where(distance == 0, send[lender, t, 0], own - 1 + distance)
            entry = jnp.where(slot < own, slot, lent)
            total[b, entry] += coef[b, k].astype(F32)
    out[...] = total[...].astype(BF16)


def weight_kernel(levels, place, vert, out):
    rows = levels * CHUNK
    total = vert.shape[0]
    lev = place[1]
    shape = (rows, total)
    pick = lax.broadcasted_iota(jnp.int32, shape, 0) // CHUNK + lev * levels
    left = (lax.broadcasted_iota(jnp.int32, shape, 1) == pick).astype(BF16)
    spread = jnp.dot(left, vert[...], preferred_element_type=F32).astype(BF16)
    row = lax.broadcasted_iota(jnp.int32, (rows, rows), 0)
    col = lax.broadcasted_iota(jnp.int32, (rows, rows), 1)
    same = lax.rem(row, CHUNK) == lax.rem(col, CHUNK)
    for side in range(2):
        base = jnp.where(lev == side, 0, levels)
        wanted = lax.broadcasted_iota(jnp.int32, shape, 0) // CHUNK + base
        right = (lax.broadcasted_iota(jnp.int32, shape, 1) == wanted).astype(BF16)
        full = dot_nt(spread, right)
        out[side] = jnp.where(same, full, 0.0).astype(BF16)


def vertical_kernel(count, weight, own, other, out):
    value = jnp.dot(weight[0], own[...], preferred_element_type=F32)
    value += jnp.dot(weight[1], other[...], preferred_element_type=F32)
    node = lax.broadcasted_iota(jnp.int32, value.shape, 1)
    out[...] = jnp.where(node < count[0], value, 0.0).astype(BF16)


def spread_kernel(
    tiles, place, send, coef_own, coef_lent, own, near, beyond, across, far, farthest, out, held, sems
):
    t, lev, sub, grp = (place[i] for i in range(4))
    inner = jnp.logical_and(t > 0, t < tiles - 1)
    blocks, _, size = held.shape[1:]

    def fetch(source, d):
        for b in range(blocks):
            part = source.at[:, pl.ds(b * size, size)]
            pltpu.make_async_copy(part, held.at[d, b], sems.at[d, b]).start()

    fetch(own, 0)
    fetch(near, 1)
    pl.when(inner)(functools.partial(fetch, beyond, 2))
    pl.when(inner)(functools.partial(fetch, across, 3))
    pl.when(jnp.logical_not(inner))(functools.partial(fetch, far, 2))
    pl.when(jnp.logical_not(inner))(functools.partial(fetch, farthest, 3))
    for d in range(tiles):
        for b in range(blocks):
            pltpu.make_async_copy(held.at[d, b], held.at[d, b], sems.at[d, b]).wait()
    for j in range(blocks + tiles - 1):
        away = max(0, j - blocks + 1)
        source = t ^ away
        total = None
        for e in range(blocks + tiles - 1):
            hop = max(0, e - blocks + 1)
            lender = source ^ hop
            if e < blocks:
                block = e
            else:
                block = send[lender, source, 0]
            distance = t ^ lender
            if j < blocks:
                matrix = coef_own[j, e]
            else:
                matrix = jnp.concatenate(
                    [
                        coef_lent[c % 2 ^ sub, c // 4 ^ grp, c // 2 % 2 ^ lev, away - 1, e]
                        for c in range(8)
                    ]
                )
            part = dot_nt(held[distance, block], matrix)
            total = part if total is None else total + part
        out[j] = total.astype(BF16)


def interp_kernel(tiles, place, send, slots, coef, field, *rest):
    out = rest[-1]
    own = field.shape[0] - tiles + 1
    t, sub = place[0], place[2]
    p = pl.program_id(0)
    total = None
    for j in range(coef.shape[2]):
        slot = slots[sub, p, j]
        lender = jnp.maximum(slot - own, 0)
        distance = t ^ lender
        lent = jnp.where(distance == 0, send[lender, t, 0], own - 1 + distance)
        entry = jnp.where(slot < own, slot, lent)
        part = dot_nt(field[entry], coef[0, 0, j])
        total = part if total is None else total + part
    out[...] = total.astype(BF16).reshape(out.shape)


def interpolate(chunk, half, tiles, place, send, slots, coef, field, shape, before):
    levels, members, points = shape
    count = coef.shape[1]
    chunks = members // 2 // CHUNK
    size = coef.shape[-1]

    def place_out(p, place, send, slots):
        sub = place[2]
        side = sub if half == 0 else 1 - sub
        return (0, side * chunks + chunk, p)

    in_specs = [
        pl.BlockSpec((1, 1) + coef.shape[2:], lambda p, *_: (0, p, 0, 0, 0)),
        pl.BlockSpec(field.shape, lambda p, *_: (0, 0, 0)),
    ]
    operands = [coef, field]
    aliases = {}
    if before is not None:
        in_specs.append(HBM)
        operands.append(before)
        aliases = {5: 0}
    return pl.pallas_call(
        functools.partial(interp_kernel, tiles),
        grid_spec=pltpu.PrefetchScalarGridSpec(
            num_scalar_prefetch=3,
            grid=(count,),
            in_specs=in_specs,
            out_specs=pl.BlockSpec((levels, CHUNK, size), place_out),
        ),
        out_shape=jax.ShapeDtypeStruct(shape, BF16),
        input_output_aliases=aliases,
        compiler_params=params(),
        name="interpolate",
    )(place, send, slots, *operands)


def local(
    control, node_count, vert_coef, send_list, conv_slots, conv_coef, interp_slots, interp_coef
):
    nodes, levels, members = control.shape
    _, blocks, taps, size, _ = conv_coef.shape
    tiles = lax.axis_size("tile")
    halves = lax.axis_size("sub")
    points = interp_coef.shape[1] * size
    t, lev, sub, grp = (lax.axis_index(n) for n in ("tile", "lev", "sub", "grp"))
    place = jnp.stack([t, lev, sub, grp]).astype(jnp.int32)
    chunks = members // CHUNK
    rows = levels * CHUNK
    entries = blocks + tiles - 1
    swap = [(0, 1), (1, 0)]

    state = control.transpose(1, 2, 0)
    mine = [state[:, c * CHUNK : (c + 1) * CHUNK].reshape(rows, nodes) for c in range(chunks)]
    theirs = [lax.ppermute(x, "lev", swap) for x in mine]

    merged = pl.pallas_call(
        functools.partial(merge_kernel, tiles),
        in_specs=[SMEM, SMEM, SMEM, VMEM],
        out_specs=VMEM,
        out_shape=jax.ShapeDtypeStruct((blocks, entries, size, size), BF16),
        scratch_shapes=[pltpu.VMEM((blocks, entries, size, size), F32)],
        compiler_params=params(),
        name="merge_taps",
    )(after(place, *mine), send_list, conv_slots, conv_coef[0])

    weight = pl.pallas_call(
        functools.partial(weight_kernel, levels),
        in_specs=[SMEM, VMEM],
        out_specs=VMEM,
        out_shape=jax.ShapeDtypeStruct((2, rows, rows), BF16),
        compiler_params=params(),
        name="level_weights",
    )(after(place, merged), vert_coef)

    vertical = [
        pl.pallas_call(
            vertical_kernel,
            in_specs=[SMEM, VMEM, VMEM, VMEM],
            out_specs=VMEM,
            out_shape=jax.ShapeDtypeStruct((rows, nodes), BF16),
            compiler_params=params(),
            name="vertical",
        )(node_count, weight, x, y)
        for x, y in zip(mine, theirs)
    ]
    near, across, beyond, far, farthest = ([None] * chunks for _ in range(5))
    edge_both = [(0, 1), (1, 0), (2, 3), (3, 2)]
    middle = [(1, 2), (2, 1)]
    edge_out = [(1, 0), (2, 3)]
    edge = []

    def edge_send(value, pairs):
        if len(edge) > 1:
            value = after(value, edge[-2])
        edge.append(lax.ppermute(value, "tile", pairs))
        return edge[-1]

    def do_near(c):
        near[c] = edge_send(vertical[c], edge_both)
        across[c] = lax.ppermute(after(vertical[c], *edge[:-1][-2:-1]), "tile", middle)
        beyond[c] = lax.ppermute(near[c], "tile", middle)

    def do_far(c):
        far[c] = edge_send(across[c], edge_out)

    def do_farthest(c):
        farthest[c] = edge_send(beyond[c], edge_out)

    do_near(0)
    do_far(0)
    for c in range(1, chunks):
        do_near(c)
        do_farthest(c - 1)
        do_far(c)
    do_farthest(chunks - 1)

    shares = lax.axis_size("grp") * lax.axis_size("lev") * halves
    share = (grp * lax.axis_size("lev") + lev) * halves + sub
    part = size // shares
    pieces = []
    for d in range(1, tiles):
        target = t ^ d
        block = send_list[t, target, 0]
        piece = lax.dynamic_slice(
            merged, (block, 0, share * part, 0), (1, entries, part, size)
        )[0]
        ring = [(i, i ^ d) for i in range(tiles)]
        pieces.append(lax.ppermute(piece, "tile", ring))
    gathered = after(jnp.stack(pieces), vertical[0])
    for axis in ("lev", "grp", "sub"):
        gathered = jnp.stack([gathered, lax.ppermute(gathered, axis, swap)])

    def spread(place, c):
        return pl.pallas_call(
            functools.partial(spread_kernel, tiles),
            in_specs=[SMEM, SMEM, VMEM, VMEM] + [HBM] * 6,
            out_specs=VMEM,
            out_shape=jax.ShapeDtypeStruct((entries, rows, size), BF16),
            scratch_shapes=[
                pltpu.VMEM((tiles, blocks, rows, size), BF16),
                pltpu.SemaphoreType.DMA((tiles, blocks)),
            ],
            compiler_params=params(),
            name="spread",
        )(place, send_list, merged, gathered, vertical[c], near[c], beyond[c], across[c], far[c], farthest[c])

    shape = (levels, halves * members, points)
    result = None
    ready = []
    for c in range(chunks):
        fields = spread(after(place, *ready), c)
        other = lax.ppermute(fields, "sub", swap)
        for half, field in enumerate((fields, other)):
            result = interpolate(
                c, half, tiles, place, send_list, interp_slots, interp_coef, field, shape, result
            )
            if half == 0:
                ready = [result]
    return result.transpose(2, 0, 1)


def plain(
    control, node_count, vert_coef, send_list, conv_slots, conv_coef, interp_slots, interp_coef
):
    node_rows, level_rows, member_rows = control.shape
    block_len = conv_coef.shape[-1]
    block_count = conv_coef.shape[1]
    columns = level_rows * member_rows
    tile_count = lax.axis_size("tile")
    halves = lax.axis_size("sub")
    tile_place = lax.axis_index("tile")
    level_place = lax.axis_index("lev")
    half_place = lax.axis_index("sub")
    position = lax.broadcasted_iota(jnp.int32, (node_rows, 1, 1), 0)
    masked = jnp.where(position < node_count[0], control, jnp.zeros_like(control))
    own_weights = lax.dynamic_slice_in_dim(vert_coef, level_place * level_rows, level_rows, 1)
    partial_value = jnp.einsum(
        "al,nlm->nam", own_weights, masked, preferred_element_type=jnp.float32
    )
    vertical = lax.psum_scatter(
        partial_value.astype(jnp.bfloat16), "lev", scatter_dimension=1, tiled=True
    )
    blocks = vertical.reshape(block_count, block_len, columns)
    incoming_ids = lax.dynamic_index_in_dim(send_list, tile_place, 1, keepdims=False)
    source_base = (jnp.arange(tile_count, dtype=jnp.int32) * block_count)[:, None]
    everything = lax.all_gather(blocks, "tile", axis=0, tiled=True)
    received = everything[source_base + incoming_ids]
    extended = jnp.concatenate([blocks, received.reshape(-1, block_len, columns)], 0)
    chosen = extended[conv_slots[0]]
    spread = jnp.einsum(
        "bkij,bkjc->bic", conv_coef[0], chosen, preferred_element_type=jnp.float32
    ).astype(jnp.bfloat16)
    spread_every = lax.all_gather(spread, "tile", axis=0, tiled=True)
    spread_lent = spread_every[source_base + incoming_ids]
    spread_ext = jnp.concatenate([spread, spread_lent.reshape(-1, block_len, columns)], 0)
    own_slots = lax.dynamic_index_in_dim(interp_slots, half_place, 0, keepdims=False)
    members_all = lax.all_gather(spread_ext, "sub", axis=2, tiled=True)
    picked = members_all[own_slots]
    result = jnp.einsum(
        "pjab,pjbc->pac", interp_coef[0], picked, preferred_element_type=jnp.float32
    )
    point_rows = result.shape[0] * block_len
    shaped = result.reshape(point_rows, halves, level_rows, member_rows)
    return (
        shaped.transpose(0, 2, 1, 3)
        .reshape(point_rows, level_rows, halves * member_rows)
        .astype(jnp.bfloat16)
    )


def solution(mesh):
    placed = (
        P("tile", "lev", ("grp", "sub")),
        P("tile"),
        P(),
        P(),
        P("tile", None, None),
        P("tile", None, None, None, None),
        P("tile", None, None),
        P(("tile", "sub"), None, None, None, None),
    )
    short = mesh.shape["tile"] == 4 and mesh.shape["lev"] == 2 and mesh.shape["sub"] == 2
    return jax.shard_map(
        local if short else plain,
        mesh=mesh,
        in_specs=placed,
        out_specs=P(("tile", "sub"), "lev", "grp"),
        check_vma=False,
    )
```

```python
import functools

import jax
import jax.numpy as jnp
from jax import lax
from jax.experimental import pallas as pl
from jax.experimental.pallas import tpu as pltpu
from jax.sharding import PartitionSpec as P

CHUNK = 16
VMEM_LIMIT = 20 * 1024 * 1024
SMEM = pl.BlockSpec(memory_space=pltpu.SMEM)
VMEM = pl.BlockSpec(memory_space=pltpu.VMEM)
HBM = pl.BlockSpec(memory_space=pl.ANY)
BF16 = jnp.bfloat16
F32 = jnp.float32


def params():
    return pltpu.CompilerParams(vmem_limit_bytes=VMEM_LIMIT)


def after(value, *others):
    return lax.optimization_barrier((value, others))[0]


def dot_nt(a, b):
    return lax.dot_general(a, b, (((1,), (1,)), ((), ())), preferred_element_type=F32)


def merge_kernel(tiles, place, send, slots, coef, out, pieces, total):
    blocks, taps = coef.shape[:2]
    own = blocks
    t = place[0]
    total[...] = jnp.zeros_like(total)
    for b in range(blocks):
        for k in range(taps):
            slot = slots[0, b, k]
            lender = jnp.maximum(slot - own, 0)
            distance = t ^ lender
            lent = jnp.where(distance == 0, send[lender, t, 0], own - 1 + distance)
            entry = jnp.where(slot < own, slot, lent)
            total[b, entry] += coef[b, k].astype(F32)
    out[...] = total[...].astype(BF16)
    part = pieces.shape[2]
    start = pl.multiple_of(place[4] * part, part)
    for d in range(1, tiles):
        pieces[d - 1] = out[send[t, t ^ d, 0], :, pl.ds(start, part), :]


def weight_kernel(levels, place, vert, out):
    rows = levels * CHUNK
    total = vert.shape[0]
    lev = place[1]
    shape = (rows, total)
    pick = lax.broadcasted_iota(jnp.int32, shape, 0) // CHUNK + lev * levels
    left = (lax.broadcasted_iota(jnp.int32, shape, 1) == pick).astype(BF16)
    spread = jnp.dot(left, vert[...], preferred_element_type=F32).astype(BF16)
    row = lax.broadcasted_iota(jnp.int32, (rows, rows), 0)
    col = lax.broadcasted_iota(jnp.int32, (rows, rows), 1)
    same = lax.rem(row, CHUNK) == lax.rem(col, CHUNK)
    for side in range(2):
        base = jnp.where(lev == side, 0, levels)
        wanted = lax.broadcasted_iota(jnp.int32, shape, 0) // CHUNK + base
        right = (lax.broadcasted_iota(jnp.int32, shape, 1) == wanted).astype(BF16)
        full = dot_nt(spread, right)
        out[side] = jnp.where(same, full, 0.0).astype(BF16)


def vertical_kernel(count, weight, own, other, out):
    value = jnp.dot(weight[0], own[...], preferred_element_type=F32)
    value += jnp.dot(weight[1], other[...], preferred_element_type=F32)
    node = lax.broadcasted_iota(jnp.int32, value.shape, 1)
    out[...] = jnp.where(node < count[0], value, 0.0).astype(BF16)


def spread_kernel(
    tiles, place, send, coef_own, coef_lent, own, near, beyond, across, far, farthest, out, held, sems
):
    t, lev, sub, grp = (place[i] for i in range(4))
    inner = jnp.logical_and(t > 0, t < tiles - 1)
    blocks, _, size = held.shape[1:]

    def fetch(source, d):
        for b in range(blocks):
            part = source.at[:, pl.ds(b * size, size)]
            pltpu.make_async_copy(part, held.at[d, b], sems.at[d, b]).start()

    fetch(own, 0)
    fetch(near, 1)
    pl.when(inner)(functools.partial(fetch, beyond, 2))
    pl.when(inner)(functools.partial(fetch, across, 3))
    pl.when(jnp.logical_not(inner))(functools.partial(fetch, far, 2))
    pl.when(jnp.logical_not(inner))(functools.partial(fetch, farthest, 3))
    for d in range(tiles):
        for b in range(blocks):
            pltpu.make_async_copy(held.at[d, b], held.at[d, b], sems.at[d, b]).wait()
    for j in range(blocks + tiles - 1):
        away = max(0, j - blocks + 1)
        source = t ^ away
        values, matrices = [], []
        for e in range(blocks + tiles - 1):
            hop = max(0, e - blocks + 1)
            lender = source ^ hop
            block = e if e < blocks else send[lender, source, 0]
            values.append(held[t ^ lender, block])
            if j < blocks:
                matrices.append(coef_own[j, e])
            else:
                pieces = [
                    coef_lent[c % 2 ^ sub, c // 2 ^ (2 * grp + lev), away - 1, e]
                    for c in range(8)
                ]
                matrices.append(jnp.concatenate(pieces))
        total = dot_nt(jnp.concatenate(values, 1), jnp.concatenate(matrices, 1))
        out[j] = total.astype(BF16)


def interp_kernel(tiles, chunk, chunks, half, level, place, send, slots, coef, field, *rest):
    out, made, done = rest[-3:]
    own = field.shape[0] - tiles + 1
    t, sub = place[0], place[2]
    side = sub if half == 0 else 1 - sub
    count, taps, size = coef.shape[1:4]
    levels, members = made.shape[:2]
    first = pl.multiple_of((side * chunks + chunk) * members, members)
    for p in range(count):
        fields, matrices = [], []
        for j in range(taps):
            slot = slots[sub, p, j]
            lender = jnp.maximum(slot - own, 0)
            distance = t ^ lender
            lent = jnp.where(distance == 0, send[lender, t, 0], own - 1 + distance)
            fields.append(field[jnp.where(slot < own, slot, lent)])
            matrices.append(coef[0, p, j])
        value = dot_nt(jnp.concatenate(fields, 1), jnp.concatenate(matrices, 1))
        made[:, :, p * size : (p + 1) * size] = value.astype(BF16).reshape(levels, members, size)
    copy = pltpu.make_async_copy(
        made, out.at[pl.ds(level, levels), pl.ds(first, members)], done
    )
    copy.start()
    copy.wait()


def interpolate(chunk, half, level, tiles, place, send, slots, coef, field, shape, before):
    count, _, size = coef.shape[1:4]
    chunks = shape[1] // 2 // CHUNK
    levels = field.shape[1] // CHUNK
    operands = [place, send, slots, coef, field]
    in_specs = [SMEM, SMEM, SMEM, VMEM, VMEM]
    aliases = {}
    if before is not None:
        aliases = {len(operands): 0}
        operands.append(before)
        in_specs.append(HBM)
    return pl.pallas_call(
        functools.partial(interp_kernel, tiles, chunk, chunks, half, level),
        in_specs=in_specs,
        out_specs=HBM,
        out_shape=jax.ShapeDtypeStruct(shape, BF16),
        scratch_shapes=[
            pltpu.VMEM((levels, CHUNK, count * size), BF16),
            pltpu.SemaphoreType.DMA,
        ],
        input_output_aliases=aliases,
        compiler_params=params(),
        name="interpolate",
    )(*operands)


def local(
    control, node_count, vert_coef, send_list, conv_slots, conv_coef, interp_slots, interp_coef
):
    nodes, levels, members = control.shape
    _, blocks, taps, size, _ = conv_coef.shape
    tiles = lax.axis_size("tile")
    halves = lax.axis_size("sub")
    points = interp_coef.shape[1] * size
    t, lev, sub, grp = (lax.axis_index(n) for n in ("tile", "lev", "sub", "grp"))
    shares = lax.axis_size("grp") * lax.axis_size("lev") * halves
    share = (grp * lax.axis_size("lev") + lev) * halves + sub
    place = jnp.stack([t, lev, sub, grp, share]).astype(jnp.int32)
    chunks = members // CHUNK
    rows = levels * CHUNK
    entries = blocks + tiles - 1
    swap = [(0, 1), (1, 0)]

    state = control.transpose(1, 2, 0)
    mine = [state[:, :CHUNK].reshape(rows, nodes)]
    state = after(state, mine[0])
    mine += [state[:, c * CHUNK : (c + 1) * CHUNK].reshape(rows, nodes) for c in range(1, chunks)]
    theirs = [lax.ppermute(x, "lev", swap) for x in mine]

    merged, pieces = pl.pallas_call(
        functools.partial(merge_kernel, tiles),
        in_specs=[SMEM, SMEM, SMEM, VMEM],
        out_specs=[VMEM, VMEM],
        out_shape=[
            jax.ShapeDtypeStruct((blocks, entries, size, size), BF16),
            jax.ShapeDtypeStruct((tiles - 1, entries, size // shares, size), BF16),
        ],
        scratch_shapes=[pltpu.VMEM((blocks, entries, size, size), F32)],
        compiler_params=params(),
        name="merge_taps",
    )(after(place, *mine), send_list, conv_slots, conv_coef[0])

    share = [
        lax.ppermute(pieces[d - 1], "tile", [(i, i ^ d) for i in range(tiles)])
        for d in range(1, tiles)
    ]
    share = jnp.stack(share)

    weight = pl.pallas_call(
        functools.partial(weight_kernel, levels),
        in_specs=[SMEM, VMEM],
        out_specs=VMEM,
        out_shape=jax.ShapeDtypeStruct((2, rows, rows), BF16),
        compiler_params=params(),
        name="level_weights",
    )(after(place, merged), vert_coef)

    vertical = [
        pl.pallas_call(
            vertical_kernel,
            in_specs=[SMEM, VMEM, VMEM, VMEM],
            out_specs=VMEM,
            out_shape=jax.ShapeDtypeStruct((rows, nodes), BF16),
            compiler_params=params(),
            name="vertical",
        )(node_count, after(weight, share), x, y)
        for x, y in zip(mine, theirs)
    ]
    near, across, beyond, far, farthest = ([None] * chunks for _ in range(5))
    edge_both = [(0, 1), (1, 0), (2, 3), (3, 2)]
    middle = [(1, 2), (2, 1)]
    edge_out = [(1, 0), (2, 3)]
    slots = []

    def slot(kind, c, *others):
        others = others + tuple(slots[-2] if len(slots) > 1 else ())
        if kind == "near":
            value = after(vertical[c], *others)
            near[c] = lax.ppermute(value, "tile", edge_both)
            across[c] = lax.ppermute(value, "tile", middle)
            slots.append((near[c], across[c]))
        elif kind == "far":
            far[c] = lax.ppermute(after(across[c], *others), "tile", edge_out)
            beyond[c] = lax.ppermute(after(near[c], *others), "tile", middle)
            slots.append((far[c], beyond[c]))
        else:
            farthest[c] = lax.ppermute(after(beyond[c], *others), "tile", edge_out)
            slots.append((farthest[c],))

    slot("near", 0)
    slot("far", 0, vertical[1])
    slot("near", 1)
    slot("farthest", 0)
    slot("near", 2)
    slot("far", 1, vertical[2])
    slot("farthest", 1)
    slot("far", 2)
    slot("farthest", 2)

    share = after(share, vertical[0])
    corner = [(0, 3), (1, 2), (2, 1), (3, 0)]
    shares = [
        share,
        lax.ppermute(share, "lev", swap),
        lax.ppermute(share, "grp", swap),
        lax.ppermute(share, ("grp", "lev"), corner),
    ]
    gathered = jnp.stack(shares)
    gathered = jnp.stack([gathered, lax.ppermute(gathered, "sub", swap)])

    def spread(place, c):
        return pl.pallas_call(
            functools.partial(spread_kernel, tiles),
            in_specs=[SMEM, SMEM, VMEM, VMEM] + [HBM] * 6,
            out_specs=VMEM,
            out_shape=jax.ShapeDtypeStruct((entries, rows, size), BF16),
            scratch_shapes=[
                pltpu.VMEM((tiles, blocks, rows, size), BF16),
                pltpu.SemaphoreType.DMA((tiles, blocks)),
            ],
            compiler_params=params(),
            name="spread",
        )(place, send_list, merged, gathered, vertical[c], near[c], beyond[c], across[c], far[c], farthest[c])

    shape = (levels, halves * members, points)
    result = None
    ready = []
    for c in range(chunks):
        fields = spread(after(place, *ready), c)
        other = lax.ppermute(fields, "sub", swap)
        for half, field in enumerate((fields, other)):
            result = interpolate(
                c, half, 0, tiles, place, send_list, interp_slots, interp_coef, field, shape, result
            )
            if half == 0:
                ready = [result]
    return result.transpose(2, 0, 1)


def plain(
    control, node_count, vert_coef, send_list, conv_slots, conv_coef, interp_slots, interp_coef
):
    node_rows, level_rows, member_rows = control.shape
    block_len = conv_coef.shape[-1]
    block_count = conv_coef.shape[1]
    columns = level_rows * member_rows
    tile_count = lax.axis_size("tile")
    halves = lax.axis_size("sub")
    tile_place = lax.axis_index("tile")
    level_place = lax.axis_index("lev")
    half_place = lax.axis_index("sub")
    position = lax.broadcasted_iota(jnp.int32, (node_rows, 1, 1), 0)
    masked = jnp.where(position < node_count[0], control, jnp.zeros_like(control))
    own_weights = lax.dynamic_slice_in_dim(vert_coef, level_place * level_rows, level_rows, 1)
    partial_value = jnp.einsum(
        "al,nlm->nam", own_weights, masked, preferred_element_type=jnp.float32
    )
    vertical = lax.psum_scatter(
        partial_value.astype(jnp.bfloat16), "lev", scatter_dimension=1, tiled=True
    )
    blocks = vertical.reshape(block_count, block_len, columns)
    incoming_ids = lax.dynamic_index_in_dim(send_list, tile_place, 1, keepdims=False)
    source_base = (jnp.arange(tile_count, dtype=jnp.int32) * block_count)[:, None]
    everything = lax.all_gather(blocks, "tile", axis=0, tiled=True)
    received = everything[source_base + incoming_ids]
    extended = jnp.concatenate([blocks, received.reshape(-1, block_len, columns)], 0)
    chosen = extended[conv_slots[0]]
    spread = jnp.einsum(
        "bkij,bkjc->bic", conv_coef[0], chosen, preferred_element_type=jnp.float32
    ).astype(jnp.bfloat16)
    spread_every = lax.all_gather(spread, "tile", axis=0, tiled=True)
    spread_lent = spread_every[source_base + incoming_ids]
    spread_ext = jnp.concatenate([spread, spread_lent.reshape(-1, block_len, columns)], 0)
    own_slots = lax.dynamic_index_in_dim(interp_slots, half_place, 0, keepdims=False)
    members_all = lax.all_gather(spread_ext, "sub", axis=2, tiled=True)
    picked = members_all[own_slots]
    result = jnp.einsum(
        "pjab,pjbc->pac", interp_coef[0], picked, preferred_element_type=jnp.float32
    )
    point_rows = result.shape[0] * block_len
    shaped = result.reshape(point_rows, halves, level_rows, member_rows)
    return (
        shaped.transpose(0, 2, 1, 3)
        .reshape(point_rows, level_rows, halves * member_rows)
        .astype(jnp.bfloat16)
    )


def solution(mesh):
    placed = (
        P("tile", "lev", ("grp", "sub")),
        P("tile"),
        P(),
        P(),
        P("tile", None, None),
        P("tile", None, None, None, None),
        P("tile", None, None),
        P(("tile", "sub"), None, None, None, None),
    )
    short = mesh.shape["tile"] == 4 and mesh.shape["lev"] == 2 and mesh.shape["sub"] == 2
    return jax.shard_map(
        local if short else plain,
        mesh=mesh,
        in_specs=placed,
        out_specs=P(("tile", "sub"), "lev", "grp"),
        check_vma=False,
    )
```

```python
import functools

import jax
import jax.numpy as jnp
from jax import lax
from jax.experimental import pallas as pl
from jax.experimental.pallas import tpu as pltpu
from jax.sharding import PartitionSpec as P

CHUNK = 16
VMEM_LIMIT = 20 * 1024 * 1024
SMEM = pl.BlockSpec(memory_space=pltpu.SMEM)
VMEM = pl.BlockSpec(memory_space=pltpu.VMEM)
HBM = pl.BlockSpec(memory_space=pl.ANY)
BF16 = jnp.bfloat16
F32 = jnp.float32


def params():
    return pltpu.CompilerParams(vmem_limit_bytes=VMEM_LIMIT)


def after(value, *others):
    return lax.optimization_barrier((value, others))[0]


def dot_nt(a, b):
    return lax.dot_general(a, b, (((1,), (1,)), ((), ())), preferred_element_type=F32)


def merge_kernel(tiles, place, send, slots, coef, out, pieces, total):
    blocks, taps = coef.shape[:2]
    own = blocks
    t = place[0]
    total[...] = jnp.zeros_like(total)
    for b in range(blocks):
        for k in range(taps):
            slot = slots[0, b, k]
            lender = jnp.maximum(slot - own, 0)
            distance = t ^ lender
            lent = jnp.where(distance == 0, send[lender, t, 0], own - 1 + distance)
            entry = jnp.where(slot < own, slot, lent)
            total[b, entry] += coef[b, k].astype(F32)
    out[...] = total[...].astype(BF16)
    part = pieces.shape[2]
    start = pl.multiple_of(place[4] * part, part)
    for d in range(1, tiles):
        pieces[d - 1] = out[send[t, t ^ d, 0], :, pl.ds(start, part), :]


def weight_kernel(levels, place, vert, out):
    rows = levels * CHUNK
    total = vert.shape[0]
    lev = place[1]
    shape = (rows, total)
    pick = lax.broadcasted_iota(jnp.int32, shape, 0) // CHUNK + lev * levels
    left = (lax.broadcasted_iota(jnp.int32, shape, 1) == pick).astype(BF16)
    spread = jnp.dot(left, vert[...], preferred_element_type=F32).astype(BF16)
    row = lax.broadcasted_iota(jnp.int32, (rows, rows), 0)
    col = lax.broadcasted_iota(jnp.int32, (rows, rows), 1)
    same = lax.rem(row, CHUNK) == lax.rem(col, CHUNK)
    for side in range(2):
        base = jnp.where(lev == side, 0, levels)
        wanted = lax.broadcasted_iota(jnp.int32, shape, 0) // CHUNK + base
        right = (lax.broadcasted_iota(jnp.int32, shape, 1) == wanted).astype(BF16)
        full = dot_nt(spread, right)
        out[side] = jnp.where(same, full, 0.0).astype(BF16)


def vertical_kernel(count, weight, own, other, out):
    value = jnp.dot(weight[0], own[...], preferred_element_type=F32)
    value += jnp.dot(weight[1], other[...], preferred_element_type=F32)
    node = lax.broadcasted_iota(jnp.int32, value.shape, 1)
    out[...] = jnp.where(node < count[0], value, 0.0).astype(BF16)


def spread_kernel(tiles, last, place, send, coef_own, coef_lent, *rest):
    blocks, entries, size, _ = coef_own.shape
    t, lev, sub, grp = (place[i] for i in range(4))
    inner = jnp.logical_and(t > 0, t < tiles - 1)
    out, held, sems = rest[-3:]
    rows = held.shape[-2]
    waits = []

    def fetch(source, d):
        for b in range(blocks):
            part = source.at[:, pl.ds(b * size, size)]
            pltpu.make_async_copy(part, held.at[d, b], sems.at[d, b]).start()

    def expect(d):
        for b in range(blocks):
            pltpu.make_async_copy(held.at[d, b], held.at[d, b], sems.at[d, b]).wait()

    known = []
    if last is not True:
        own, near, beyond, far = rest[:4]
        fetch(own, 0)
        fetch(near, 1)
        pl.when(inner)(functools.partial(fetch, beyond, 2))
        pl.when(jnp.logical_not(inner))(functools.partial(fetch, far, 2))
        known = [0, 1, 2]
    if last is not False:
        across, farthest = rest[-5:-3]
        pl.when(inner)(functools.partial(fetch, across, 3))
        pl.when(jnp.logical_not(inner))(functools.partial(fetch, farthest, 3))
        known.append(3)
    for d in known:
        expect(d)
    for j in range(entries):
        away = max(0, j - blocks + 1)
        source = t ^ away
        values, matrices = [], []
        for e in range(entries):
            hop = max(0, e - blocks + 1)
            if away ^ hop not in known:
                continue
            lender = source ^ hop
            block = e if e < blocks else send[lender, source, 0]
            values.append(held[away ^ hop, block])
            if j < blocks:
                matrices.append(coef_own[j, e])
            else:
                pieces = [
                    coef_lent[c % 2 ^ sub, c // 2 ^ (2 * grp + lev), away - 1, e]
                    for c in range(8)
                ]
                matrices.append(jnp.concatenate(pieces))
        total = dot_nt(jnp.concatenate(values, 1), jnp.concatenate(matrices, 1))
        if last is True:
            total += rest[0][j]
        out[j] = total.astype(out.dtype)


def interp_kernel(tiles, chunks, jobs, place, send, slots, coef, *rest):
    out, made, sems = rest[-3:]
    t, sub = place[0], place[2]
    levels, members = made.shape[1:3]
    own = rest[0].shape[0] - tiles + 1
    size = coef.shape[-1]
    copies = []
    for i, (chunk, half) in enumerate(jobs):
        field = rest[i]
        side = sub if half == 0 else 1 - sub
        first = pl.multiple_of((side * chunks + chunk) * members, members)
        for p in range(coef.shape[1]):
            fields, matrices = [], []
            for j in range(coef.shape[2]):
                slot = slots[sub, p, j]
                lender = jnp.maximum(slot - own, 0)
                distance = t ^ lender
                lent = jnp.where(distance == 0, send[lender, t, 0], own - 1 + distance)
                fields.append(field[jnp.where(slot < own, slot, lent)])
                matrices.append(coef[0, p, j])
            value = dot_nt(jnp.concatenate(fields, 1), jnp.concatenate(matrices, 1))
            value = value.astype(BF16).reshape(levels, members, size)
            made[i, :, :, p * size : (p + 1) * size] = value
        copies.append(
            pltpu.make_async_copy(made.at[i], out.at[:, pl.ds(first, members)], sems.at[i])
        )
        copies[-1].start()
    for copy in copies:
        copy.wait()


def interpolate(jobs, tiles, place, send, slots, coef, fields, shape, before):
    levels, members, points = shape
    operands = [place, send, slots, coef, *fields]
    in_specs = [SMEM, SMEM, SMEM, VMEM] + [VMEM] * len(fields)
    aliases = {}
    if before is not None:
        aliases = {len(operands): 0}
        operands.append(before)
        in_specs.append(HBM)
    return pl.pallas_call(
        functools.partial(interp_kernel, tiles, members // 2 // CHUNK, jobs),
        in_specs=in_specs,
        out_specs=HBM,
        out_shape=jax.ShapeDtypeStruct(shape, BF16),
        scratch_shapes=[
            pltpu.VMEM((len(jobs), levels, CHUNK, points), BF16),
            pltpu.SemaphoreType.DMA((len(jobs),)),
        ],
        input_output_aliases=aliases,
        compiler_params=params(),
        name="interpolate",
    )(*operands)


def local(
    control, node_count, vert_coef, send_list, conv_slots, conv_coef, interp_slots, interp_coef
):
    nodes, levels, members = control.shape
    _, blocks, taps, size, _ = conv_coef.shape
    tiles = lax.axis_size("tile")
    halves = lax.axis_size("sub")
    points = interp_coef.shape[1] * size
    t, lev, sub, grp = (lax.axis_index(n) for n in ("tile", "lev", "sub", "grp"))
    shares = lax.axis_size("grp") * lax.axis_size("lev") * halves
    share = (grp * lax.axis_size("lev") + lev) * halves + sub
    place = jnp.stack([t, lev, sub, grp, share]).astype(jnp.int32)
    chunks = members // CHUNK
    rows = levels * CHUNK
    entries = blocks + tiles - 1
    swap = [(0, 1), (1, 0)]

    state = control.transpose(1, 2, 0)
    mine = [state[:, :CHUNK].reshape(rows, nodes)]
    state = after(state, mine[0])
    mine += [state[:, c * CHUNK : (c + 1) * CHUNK].reshape(rows, nodes) for c in range(1, chunks)]
    theirs = [lax.ppermute(x, "lev", swap) for x in mine]

    merged, pieces = pl.pallas_call(
        functools.partial(merge_kernel, tiles),
        in_specs=[SMEM, SMEM, SMEM, VMEM],
        out_specs=[VMEM, VMEM],
        out_shape=[
            jax.ShapeDtypeStruct((blocks, entries, size, size), BF16),
            jax.ShapeDtypeStruct((tiles - 1, entries, size // shares, size), BF16),
        ],
        scratch_shapes=[pltpu.VMEM((blocks, entries, size, size), F32)],
        compiler_params=params(),
        name="merge_taps",
    )(after(place, *mine), send_list, conv_slots, conv_coef[0])

    share = [
        lax.ppermute(pieces[d - 1], "tile", [(i, i ^ d) for i in range(tiles)])
        for d in range(1, tiles)
    ]
    share = jnp.stack(share)

    weight = pl.pallas_call(
        functools.partial(weight_kernel, levels),
        in_specs=[SMEM, VMEM],
        out_specs=VMEM,
        out_shape=jax.ShapeDtypeStruct((2, rows, rows), BF16),
        compiler_params=params(),
        name="level_weights",
    )(after(place, merged), vert_coef)

    vertical = [
        pl.pallas_call(
            vertical_kernel,
            in_specs=[SMEM, VMEM, VMEM, VMEM],
            out_specs=VMEM,
            out_shape=jax.ShapeDtypeStruct((rows, nodes), BF16),
            compiler_params=params(),
            name="vertical",
        )(node_count, after(weight, share), x, y)
        for x, y in zip(mine, theirs)
    ]
    near, across, beyond, far, farthest = ([None] * chunks for _ in range(5))
    edge_both = [(0, 1), (1, 0), (2, 3), (3, 2)]
    middle = [(1, 2), (2, 1)]
    edge_out = [(1, 0), (2, 3)]
    slots = []

    def slot(kind, c, *others):
        others = others + tuple(slots[-2] if len(slots) > 1 else ())
        if kind == "near":
            value = after(vertical[c], *others)
            near[c] = lax.ppermute(value, "tile", edge_both)
            across[c] = lax.ppermute(value, "tile", middle)
            slots.append((near[c], across[c]))
        elif kind == "far":
            far[c] = lax.ppermute(after(across[c], *others), "tile", edge_out)
            beyond[c] = lax.ppermute(after(near[c], *others), "tile", middle)
            slots.append((far[c], beyond[c]))
        else:
            farthest[c] = lax.ppermute(after(beyond[c], *others), "tile", edge_out)
            slots.append((farthest[c],))

    slot("near", 0)
    slot("far", 0, vertical[1])
    slot("near", 1)
    slot("farthest", 0)
    slot("near", 2)
    slot("far", 1, vertical[2])
    slot("farthest", 1)
    slot("far", 2)
    slot("farthest", 2)

    share = after(share, vertical[0])
    corner = [(0, 3), (1, 2), (2, 1), (3, 0)]
    shares = [
        share,
        lax.ppermute(share, "lev", swap),
        lax.ppermute(share, "grp", swap),
        lax.ppermute(share, ("grp", "lev"), corner),
    ]
    gathered = jnp.stack(shares)
    gathered = jnp.stack([gathered, lax.ppermute(gathered, "sub", swap)])

    def spread(place, c, last, *sources):
        count = len(sources) - (last is True)
        return pl.pallas_call(
            functools.partial(spread_kernel, tiles, last),
            in_specs=[SMEM, SMEM, VMEM, VMEM]
            + [VMEM] * (len(sources) - count)
            + [HBM] * count,
            out_specs=VMEM,
            out_shape=jax.ShapeDtypeStruct((entries, rows, size), F32 if last is False else BF16),
            scratch_shapes=[
                pltpu.VMEM((tiles, blocks, rows, size), BF16),
                pltpu.SemaphoreType.DMA((tiles, blocks)),
            ],
            compiler_params=params(),
            name="spread",
        )(place, send_list, merged, gathered, *sources)

    shape = (levels, halves * members, points)

    def flush(jobs, result):
        which, fields = zip(*jobs)
        return interpolate(
            which, tiles, place, send_list, interp_slots, interp_coef, fields, shape, result
        )

    result = None
    ready = []
    jobs = []
    for c in range(chunks):
        held = after(place, *ready)
        early = (vertical[c], near[c], beyond[c], far[c])
        late = (across[c], farthest[c])
        if c + 1 < chunks:
            fields = spread(held, c, None, *early, *late)
        else:
            fields = spread(held, c, True, spread(held, c, False, *early), *late)
        jobs.append(((c, 0), fields))
        result = flush(jobs, result)
        ready = [result]
        jobs = [((c, 1), lax.ppermute(fields, "sub", swap))]
    result = flush(jobs, result)
    return result.transpose(2, 0, 1)


def plain(
    control, node_count, vert_coef, send_list, conv_slots, conv_coef, interp_slots, interp_coef
):
    node_rows, level_rows, member_rows = control.shape
    block_len = conv_coef.shape[-1]
    block_count = conv_coef.shape[1]
    columns = level_rows * member_rows
    tile_count = lax.axis_size("tile")
    halves = lax.axis_size("sub")
    tile_place = lax.axis_index("tile")
    level_place = lax.axis_index("lev")
    half_place = lax.axis_index("sub")
    position = lax.broadcasted_iota(jnp.int32, (node_rows, 1, 1), 0)
    masked = jnp.where(position < node_count[0], control, jnp.zeros_like(control))
    own_weights = lax.dynamic_slice_in_dim(vert_coef, level_place * level_rows, level_rows, 1)
    partial_value = jnp.einsum(
        "al,nlm->nam", own_weights, masked, preferred_element_type=jnp.float32
    )
    vertical = lax.psum_scatter(
        partial_value.astype(jnp.bfloat16), "lev", scatter_dimension=1, tiled=True
    )
    blocks = vertical.reshape(block_count, block_len, columns)
    incoming_ids = lax.dynamic_index_in_dim(send_list, tile_place, 1, keepdims=False)
    source_base = (jnp.arange(tile_count, dtype=jnp.int32) * block_count)[:, None]
    everything = lax.all_gather(blocks, "tile", axis=0, tiled=True)
    received = everything[source_base + incoming_ids]
    extended = jnp.concatenate([blocks, received.reshape(-1, block_len, columns)], 0)
    chosen = extended[conv_slots[0]]
    spread = jnp.einsum(
        "bkij,bkjc->bic", conv_coef[0], chosen, preferred_element_type=jnp.float32
    ).astype(jnp.bfloat16)
    spread_every = lax.all_gather(spread, "tile", axis=0, tiled=True)
    spread_lent = spread_every[source_base + incoming_ids]
    spread_ext = jnp.concatenate([spread, spread_lent.reshape(-1, block_len, columns)], 0)
    own_slots = lax.dynamic_index_in_dim(interp_slots, half_place, 0, keepdims=False)
    members_all = lax.all_gather(spread_ext, "sub", axis=2, tiled=True)
    picked = members_all[own_slots]
    result = jnp.einsum(
        "pjab,pjbc->pac", interp_coef[0], picked, preferred_element_type=jnp.float32
    )
    point_rows = result.shape[0] * block_len
    shaped = result.reshape(point_rows, halves, level_rows, member_rows)
    return (
        shaped.transpose(0, 2, 1, 3)
        .reshape(point_rows, level_rows, halves * member_rows)
        .astype(jnp.bfloat16)
    )


def solution(mesh):
    placed = (
        P("tile", "lev", ("grp", "sub")),
        P("tile"),
        P(),
        P(),
        P("tile", None, None),
        P("tile", None, None, None, None),
        P("tile", None, None),
        P(("tile", "sub"), None, None, None, None),
    )
    short = mesh.shape["tile"] == 4 and mesh.shape["lev"] == 2 and mesh.shape["sub"] == 2
    return jax.shard_map(
        local if short else plain,
        mesh=mesh,
        in_specs=placed,
        out_specs=P(("tile", "sub"), "lev", "grp"),
        check_vma=False,
    )
```

```python
import functools

import jax
import jax.numpy as jnp
from jax import lax
from jax.experimental import pallas as pl
from jax.experimental.pallas import tpu as pltpu
from jax.sharding import PartitionSpec as P

CHUNK = 16
VMEM_LIMIT = 20 * 1024 * 1024
SMEM = pl.BlockSpec(memory_space=pltpu.SMEM)
VMEM = pl.BlockSpec(memory_space=pltpu.VMEM)
HBM = pl.BlockSpec(memory_space=pl.ANY)
BF16 = jnp.bfloat16
F32 = jnp.float32


def params():
    return pltpu.CompilerParams(vmem_limit_bytes=VMEM_LIMIT)


def after(value, *others):
    return lax.optimization_barrier((value, others))[0]


def dot_nt(a, b):
    return lax.dot_general(a, b, (((1,), (1,)), ((), ())), preferred_element_type=F32)


def merge_kernel(tiles, place, send, slots, coef, out, pieces, total):
    blocks, taps = coef.shape[:2]
    own = blocks
    t = place[0]
    total[...] = jnp.zeros_like(total)
    for b in range(blocks):
        for k in range(taps):
            slot = slots[0, b, k]
            lender = jnp.maximum(slot - own, 0)
            distance = t ^ lender
            lent = jnp.where(distance == 0, send[lender, t, 0], own - 1 + distance)
            entry = jnp.where(slot < own, slot, lent)
            total[b, entry] += coef[b, k].astype(F32)
    out[...] = total[...].astype(BF16)
    part = pieces.shape[2]
    start = pl.multiple_of(place[4] * part, part)
    for d in range(1, tiles):
        pieces[d - 1] = out[send[t, t ^ d, 0], :, pl.ds(start, part), :]


def weight_kernel(levels, place, vert, out):
    rows = levels * CHUNK
    total = vert.shape[0]
    lev = place[1]
    shape = (rows, total)
    pick = lax.broadcasted_iota(jnp.int32, shape, 0) // CHUNK + lev * levels
    left = (lax.broadcasted_iota(jnp.int32, shape, 1) == pick).astype(BF16)
    spread = jnp.dot(left, vert[...], preferred_element_type=F32).astype(BF16)
    row = lax.broadcasted_iota(jnp.int32, (rows, rows), 0)
    col = lax.broadcasted_iota(jnp.int32, (rows, rows), 1)
    same = lax.rem(row, CHUNK) == lax.rem(col, CHUNK)
    for side in range(2):
        base = jnp.where(lev == side, 0, levels)
        wanted = lax.broadcasted_iota(jnp.int32, shape, 0) // CHUNK + base
        right = (lax.broadcasted_iota(jnp.int32, shape, 1) == wanted).astype(BF16)
        full = dot_nt(spread, right)
        out[side] = jnp.where(same, full, 0.0).astype(BF16)


def vertical_kernel(count, weight, own, other, out):
    value = jnp.dot(weight[0], own[...], preferred_element_type=F32)
    value += jnp.dot(weight[1], other[...], preferred_element_type=F32)
    node = lax.broadcasted_iota(jnp.int32, value.shape, 1)
    out[...] = jnp.where(node < count[0], value, 0.0).astype(BF16)


def spread_kernel(tiles, last, place, send, coef_own, coef_lent, *rest):
    blocks, entries, size, _ = coef_own.shape
    t, lev, sub, grp = (place[i] for i in range(4))
    inner = jnp.logical_and(t > 0, t < tiles - 1)
    out, held, sems = rest[-3:]
    rows = held.shape[-2]
    waits = []

    def fetch(source, d):
        for b in range(blocks):
            part = source.at[:, pl.ds(b * size, size)]
            pltpu.make_async_copy(part, held.at[d, b], sems.at[d, b]).start()

    def expect(d):
        for b in range(blocks):
            pltpu.make_async_copy(held.at[d, b], held.at[d, b], sems.at[d, b]).wait()

    known = []
    if last is not True:
        own, near, beyond, far = rest[:4]
        fetch(own, 0)
        fetch(near, 1)
        pl.when(inner)(functools.partial(fetch, beyond, 2))
        pl.when(jnp.logical_not(inner))(functools.partial(fetch, far, 2))
        known = [0, 1, 2]
    if last is not False:
        across, farthest = rest[-5:-3]
        pl.when(inner)(functools.partial(fetch, across, 3))
        pl.when(jnp.logical_not(inner))(functools.partial(fetch, farthest, 3))
        known.append(3)
    for d in known:
        expect(d)
    for j in range(entries):
        away = max(0, j - blocks + 1)
        source = t ^ away
        values, matrices = [], []
        for e in range(entries):
            hop = max(0, e - blocks + 1)
            if away ^ hop not in known:
                continue
            lender = source ^ hop
            block = e if e < blocks else send[lender, source, 0]
            values.append(held[away ^ hop, block])
            if j < blocks:
                matrices.append(coef_own[j, e])
            else:
                pieces = [
                    coef_lent[c % 2 ^ sub, c // 2 ^ (2 * grp + lev), away - 1, e]
                    for c in range(8)
                ]
                matrices.append(jnp.concatenate(pieces))
        total = dot_nt(jnp.concatenate(values, 1), jnp.concatenate(matrices, 1))
        if last is True:
            total += rest[0][j]
        out[j] = total.astype(out.dtype)


def interp_kernel(tiles, chunks, jobs, place, send, slots, coef, *rest):
    out, made, sems = rest[-3:]
    t, sub = place[0], place[2]
    levels, members = made.shape[1:3]
    own = rest[0].shape[0] - tiles + 1
    size = coef.shape[-1]
    copies = []
    for i, (chunk, half) in enumerate(jobs):
        field = rest[i]
        side = sub if half == 0 else 1 - sub
        first = pl.multiple_of((side * chunks + chunk) * members, members)
        for p in range(coef.shape[1]):
            fields, matrices = [], []
            for j in range(coef.shape[2]):
                slot = slots[sub, p, j]
                lender = jnp.maximum(slot - own, 0)
                distance = t ^ lender
                lent = jnp.where(distance == 0, send[lender, t, 0], own - 1 + distance)
                fields.append(field[jnp.where(slot < own, slot, lent)])
                matrices.append(coef[0, p, j])
            value = dot_nt(jnp.concatenate(fields, 1), jnp.concatenate(matrices, 1))
            value = value.astype(BF16).reshape(levels, members, size)
            made[i, :, :, p * size : (p + 1) * size] = value
        copies.append(
            pltpu.make_async_copy(made.at[i], out.at[:, pl.ds(first, members)], sems.at[i])
        )
        copies[-1].start()
    for copy in copies:
        copy.wait()


def interpolate(jobs, tiles, place, send, slots, coef, fields, shape, before):
    levels, members, points = shape
    operands = [place, send, slots, coef, *fields]
    in_specs = [SMEM, SMEM, SMEM, VMEM] + [VMEM] * len(fields)
    aliases = {}
    if before is not None:
        aliases = {len(operands): 0}
        operands.append(before)
        in_specs.append(HBM)
    return pl.pallas_call(
        functools.partial(interp_kernel, tiles, members // 2 // CHUNK, jobs),
        in_specs=in_specs,
        out_specs=HBM,
        out_shape=jax.ShapeDtypeStruct(shape, BF16),
        scratch_shapes=[
            pltpu.VMEM((len(jobs), levels, CHUNK, points), BF16),
            pltpu.SemaphoreType.DMA((len(jobs),)),
        ],
        input_output_aliases=aliases,
        compiler_params=params(),
        name="interpolate",
    )(*operands)


def local(
    control, node_count, vert_coef, send_list, conv_slots, conv_coef, interp_slots, interp_coef
):
    nodes, levels, members = control.shape
    _, blocks, taps, size, _ = conv_coef.shape
    tiles = lax.axis_size("tile")
    halves = lax.axis_size("sub")
    points = interp_coef.shape[1] * size
    t, lev, sub, grp = (lax.axis_index(n) for n in ("tile", "lev", "sub", "grp"))
    shares = lax.axis_size("grp") * lax.axis_size("lev") * halves
    share = (grp * lax.axis_size("lev") + lev) * halves + sub
    place = jnp.stack([t, lev, sub, grp, share]).astype(jnp.int32)
    chunks = members // CHUNK
    rows = levels * CHUNK
    entries = blocks + tiles - 1
    swap = [(0, 1), (1, 0)]

    state = control.transpose(1, 2, 0)
    mine = [state[:, :CHUNK].reshape(rows, nodes)]
    state = after(state, mine[0])
    valid = lax.broadcasted_iota(jnp.int32, (levels, CHUNK, nodes), 2) < node_count[0]
    parts = [state[:, c * CHUNK : (c + 1) * CHUNK] for c in range(1, chunks)]
    parts[-1] = jnp.where(valid, parts[-1], 0)
    mine += [x.reshape(rows, nodes) for x in parts]
    edge_both = [(0, 1), (1, 0), (2, 3), (3, 2)]
    raw = lax.ppermute(mine[-1], "tile", edge_both)
    theirs = [lax.ppermute(mine[0], "lev", swap)]

    merged, pieces = pl.pallas_call(
        functools.partial(merge_kernel, tiles),
        in_specs=[SMEM, SMEM, SMEM, VMEM],
        out_specs=[VMEM, VMEM],
        out_shape=[
            jax.ShapeDtypeStruct((blocks, entries, size, size), BF16),
            jax.ShapeDtypeStruct((tiles - 1, entries, size // shares, size), BF16),
        ],
        scratch_shapes=[pltpu.VMEM((blocks, entries, size, size), F32)],
        compiler_params=params(),
        name="merge_taps",
    )(after(place, *mine), send_list, conv_slots, conv_coef[0])

    share = [
        lax.ppermute(pieces[d - 1], "tile", [(i, i ^ d) for i in range(tiles)])
        for d in range(1, tiles)
    ]
    share = jnp.stack(share)

    weight = pl.pallas_call(
        functools.partial(weight_kernel, levels),
        in_specs=[SMEM, VMEM],
        out_specs=VMEM,
        out_shape=jax.ShapeDtypeStruct((2, rows, rows), BF16),
        compiler_params=params(),
        name="level_weights",
    )(after(place, merged), vert_coef)

    theirs += [lax.ppermute(after(x, share), "lev", swap) for x in mine[1:]]

    def do_vertical(count, x, y, *others):
        return pl.pallas_call(
            vertical_kernel,
            in_specs=[SMEM, VMEM, VMEM, VMEM],
            out_specs=VMEM,
            out_shape=jax.ShapeDtypeStruct((rows, nodes), BF16),
            compiler_params=params(),
            name="vertical",
        )(count, after(weight, *others), x, y)

    vertical = [do_vertical(node_count, x, y, share, *([raw] if i else [])) for i, (x, y) in enumerate(zip(mine, theirs))]
    raw_other = lax.ppermute(after(raw, theirs[-1]), "lev", swap)
    everywhere = jnp.full((1,), nodes, jnp.int32)

    near, across, beyond, far, farthest = ([None] * chunks for _ in range(5))
    middle = [(1, 2), (2, 1)]
    edge_out = [(1, 0), (2, 3)]
    slots = []

    def slot(kind, c, *others):
        others = others + tuple(slots[-2] if len(slots) > 1 else ())
        if kind == "near":
            value = after(vertical[c], *others)
            across[c] = lax.ppermute(value, "tile", middle)
            if c + 1 == chunks:
                near[c] = do_vertical(everywhere, raw, raw_other)
                return
            near[c] = lax.ppermute(value, "tile", edge_both)
            slots.append((near[c], across[c]))
        elif kind == "far":
            far[c] = lax.ppermute(after(across[c], *others), "tile", edge_out)
            beyond[c] = lax.ppermute(after(near[c], *others), "tile", middle)
            slots.append((far[c], beyond[c]))
        else:
            farthest[c] = lax.ppermute(after(beyond[c], *others), "tile", edge_out)
            slots.append((farthest[c],))

    slot("near", 0)
    slot("far", 0, vertical[1])
    slot("near", 1)
    slot("farthest", 0)
    slot("far", 1, vertical[2])
    slot("near", 2)
    slot("farthest", 1, near[2])
    slot("far", 2)
    slot("farthest", 2)

    share = after(share, vertical[0])
    corner = [(0, 3), (1, 2), (2, 1), (3, 0)]
    shares = [
        share,
        lax.ppermute(share, "lev", swap),
        lax.ppermute(share, "grp", swap),
        lax.ppermute(share, ("grp", "lev"), corner),
    ]
    gathered = jnp.stack(shares)
    gathered = jnp.stack([gathered, lax.ppermute(gathered, "sub", swap)])

    def spread(place, c, last, *sources):
        count = len(sources) - (last is True)
        return pl.pallas_call(
            functools.partial(spread_kernel, tiles, last),
            in_specs=[SMEM, SMEM, VMEM, VMEM]
            + [VMEM] * (len(sources) - count)
            + [HBM] * count,
            out_specs=VMEM,
            out_shape=jax.ShapeDtypeStruct((entries, rows, size), F32 if last is False else BF16),
            scratch_shapes=[
                pltpu.VMEM((tiles, blocks, rows, size), BF16),
                pltpu.SemaphoreType.DMA((tiles, blocks)),
            ],
            compiler_params=params(),
            name="spread",
        )(place, send_list, merged, gathered, *sources)

    shape = (levels, halves * members, points)

    def flush(jobs, result):
        which, fields = zip(*jobs)
        return interpolate(
            which, tiles, place, send_list, interp_slots, interp_coef, fields, shape, result
        )

    result = None
    ready = []
    jobs = []
    for c in range(chunks):
        held = after(place, *ready)
        early = (vertical[c], near[c], beyond[c], far[c])
        late = (across[c], farthest[c])
        if c + 1 < chunks:
            fields = spread(held, c, None, *early, *late)
        else:
            fields = spread(held, c, True, spread(held, c, False, *early), *late)
        jobs.append(((c, 0), fields))
        result = flush(jobs, result)
        ready = [result]
        jobs = [((c, 1), lax.ppermute(fields, "sub", swap))]
    result = flush(jobs, result)
    return result.transpose(2, 0, 1)


def plain(
    control, node_count, vert_coef, send_list, conv_slots, conv_coef, interp_slots, interp_coef
):
    node_rows, level_rows, member_rows = control.shape
    block_len = conv_coef.shape[-1]
    block_count = conv_coef.shape[1]
    columns = level_rows * member_rows
    tile_count = lax.axis_size("tile")
    halves = lax.axis_size("sub")
    tile_place = lax.axis_index("tile")
    level_place = lax.axis_index("lev")
    half_place = lax.axis_index("sub")
    position = lax.broadcasted_iota(jnp.int32, (node_rows, 1, 1), 0)
    masked = jnp.where(position < node_count[0], control, jnp.zeros_like(control))
    own_weights = lax.dynamic_slice_in_dim(vert_coef, level_place * level_rows, level_rows, 1)
    partial_value = jnp.einsum(
        "al,nlm->nam", own_weights, masked, preferred_element_type=jnp.float32
    )
    vertical = lax.psum_scatter(
        partial_value.astype(jnp.bfloat16), "lev", scatter_dimension=1, tiled=True
    )
    blocks = vertical.reshape(block_count, block_len, columns)
    incoming_ids = lax.dynamic_index_in_dim(send_list, tile_place, 1, keepdims=False)
    source_base = (jnp.arange(tile_count, dtype=jnp.int32) * block_count)[:, None]
    everything = lax.all_gather(blocks, "tile", axis=0, tiled=True)
    received = everything[source_base + incoming_ids]
    extended = jnp.concatenate([blocks, received.reshape(-1, block_len, columns)], 0)
    chosen = extended[conv_slots[0]]
    spread = jnp.einsum(
        "bkij,bkjc->bic", conv_coef[0], chosen, preferred_element_type=jnp.float32
    ).astype(jnp.bfloat16)
    spread_every = lax.all_gather(spread, "tile", axis=0, tiled=True)
    spread_lent = spread_every[source_base + incoming_ids]
    spread_ext = jnp.concatenate([spread, spread_lent.reshape(-1, block_len, columns)], 0)
    own_slots = lax.dynamic_index_in_dim(interp_slots, half_place, 0, keepdims=False)
    members_all = lax.all_gather(spread_ext, "sub", axis=2, tiled=True)
    picked = members_all[own_slots]
    result = jnp.einsum(
        "pjab,pjbc->pac", interp_coef[0], picked, preferred_element_type=jnp.float32
    )
    point_rows = result.shape[0] * block_len
    shaped = result.reshape(point_rows, halves, level_rows, member_rows)
    return (
        shaped.transpose(0, 2, 1, 3)
        .reshape(point_rows, level_rows, halves * member_rows)
        .astype(jnp.bfloat16)
    )


def solution(mesh):
    placed = (
        P("tile", "lev", ("grp", "sub")),
        P("tile"),
        P(),
        P(),
        P("tile", None, None),
        P("tile", None, None, None, None),
        P("tile", None, None),
        P(("tile", "sub"), None, None, None, None),
    )
    short = mesh.shape["tile"] == 4 and mesh.shape["lev"] == 2 and mesh.shape["sub"] == 2
    return jax.shard_map(
        local if short else plain,
        mesh=mesh,
        in_specs=placed,
        out_specs=P(("tile", "sub"), "lev", "grp"),
        check_vma=False,
    )
```
